32 devices in a mesh: grp: 2 (over y), req: 4 (over z), tp: 4 (over x, core).
Axes of the slice: x: 2, y: 2, z: 4, core: 2. Of those that a mesh axis runs over, the one named last changes fastest.
Arguments:
- queries: bfloat16 [8, 256, 64, 128], P(('grp', 'req'), None, 'tp'), parts along dimension 0, may hold values from -200 to 200
- kv_new: bfloat16 [8, 256, 2, 8, 128], P(('grp', 'req'), None, None, 'tp'), parts along dimension 0, may hold values from -4 to 4
- kv_codes: bfloat16 [64, 2, 8, 128, 128], P(('grp', 'req'), None, 'tp'), parts along dimension 0, may hold values from -4 to 4
- kv_scale: bfloat16 [64, 2, 8, 128], P(('grp', 'req'), None, 'tp'), parts along dimension 0, may hold values from 0.5 to 2
- block_owner: int32 [8, 24], P('grp'), parts along dimension 0, may hold values from 0 to 3, as said below
- block_index: int32 [8, 24], P('grp'), parts along dimension 0, may hold values from 0 to 7
- prefix_blocks: int32 [8], P('grp'), parts along dimension 0, may hold values from 1 to 24, as said below
- state_owner: int32 [8], P('grp'), parts along dimension 0, may hold values from 0 to 3, as said below
- ssm_pool: float32 [8, 128, 64, 256], P(('grp', 'req'), 'tp'), parts along dimension 0, may hold values from -0.375 to 0.375
- conv_pool_x: bfloat16 [8, 3, 8192], P(('grp', 'req'), None, 'tp'), parts along dimension 0, may hold values from -4 to 4
- conv_pool_bc: bfloat16 [8, 3, 2, 2048], P(('grp', 'req'), None, None, 'tp'), parts along dimension 0, may hold values from -4 to 4
- x_in: bfloat16 [8, 256, 8192], P(('grp', 'req'), None, 'tp'), parts along dimension 0, may hold values from -5 to 5
- bc_in: bfloat16 [8, 256, 2, 2048], P(('grp', 'req'), None, None, 'tp'), parts along dimension 0, may hold values from -5 to 5
- z_in: bfloat16 [8, 256, 8192], P(('grp', 'req'), None, 'tp'), parts along dimension 0, may hold values from -5 to 5
- dt_raw: float32 [8, 256, 128], P(('grp', 'req'), None, 'tp'), parts along dimension 0, may hold values from -5 to 5
- dt_bias: float32 [128], P('tp'), may hold values from -4 to -2
- ssm_rate: float32 [128], P('tp'), may hold values from 0.03 to 1
- skip_gain: float32 [128], P('tp'), may hold values from 0.5 to 1.5
- conv_weight_x: bfloat16 [4, 8192], P(None, 'tp'), may hold values from -3 to 3
- conv_weight_bc: bfloat16 [4, 2, 2048], P(None, None, 'tp'), may hold values from -3 to 3
- conv_bias_x: bfloat16 [8192], P('tp'), may hold values from -2.5 to 2.5
- conv_bias_bc: bfloat16 [2, 2048], P(None, 'tp'), may hold values from -2.5 to 2.5
- norm_gain: bfloat16 [8192], P('tp'), may hold values from 0.099609375 to 1.8984375
Outputs:
- ssm_out: bfloat16 [8, 256, 8192], P(('grp', 'req'), None, 'tp'), parts along dimension 0
- attn_out: bfloat16 [8, 256, 64, 128], P(('grp', 'req'), None, 'tp'), parts along dimension 0
The draws below stay inside these ranges and needn't reach their ends.
There are 2 independent parts, one for each index of `grp`. The reference program is written for one: setup_inputs(seed, part) draws one part's arguments, and reference() takes and returns one part's arrays. A program takes and returns all parts, laid end to end along the dimension named above; an argument that names none is the same for every part. Nothing has to cross between parts.
Inputs may be any that keep to these rules, and one draw needn't show every extreme that they name: `block_owner`: entries name devices along req. At most 6 of the 24 entries of one request name the same owner, and in every draw some owner is named exactly 6 times by every request. Only the first prefix_blocks[r] entries of request r's table belong to its prefix; the other entries are unused. `state_owner`: A permutation: each owner holds the cached states of exactly one request.
All inputs are finite; a program needn't handle non-finite values.
Results may differ from the reference program's by a relative error of at most 0.0073.
Values may be sent and summed in bfloat16 or wider, within the bound.
A program may use at most 64 MiB of HBM per device.

```python
import math
import jax
import jax.numpy as jnp
from jax import lax

H = 128
P_SIZE = 64
N = 256
G = 8
CONV_K = 4
QH = 64
KVH = 8
HD = 128
BLK = 128
L = 256
MAXB = 24
NB_DEV = 8
REQS = 4
POOL = 32
CAP = 6
N_REQ = 4


def shared_heads(key):
    return jnp.clip(jax.random.normal(key, (REQS, L, 2, KVH, HD), jnp.float32), -3.0, 3.0)


def draw_kv_new(key, part):
    values = shared_heads(key)
    return values.astype(jnp.bfloat16)


def draw_queries(key, part):
    key = jax.random.fold_in(key, 5)
    queries = jnp.clip(jax.random.normal(key, (REQS, L, QH, HD), jnp.float32), -3.0, 3.0)
    return queries.astype(jnp.bfloat16)


def one_order(inner_key):
    return jax.random.permutation(inner_key, N_REQ).astype(jnp.int32)


def place_owner(orders, row, value, position, common):
    row_vals = orders[row]
    where_value = jnp.argmax((row_vals == value).astype(jnp.int32)).astype(jnp.int32)
    old_value = row_vals[position]
    swapped = row_vals.at[where_value].set(old_value).at[position].set(value)
    kept = jnp.where(value == common, row_vals, swapped)
    return orders.at[row].set(kept)


def draw_block_owner(key, part):
    key = jax.random.fold_in(key, 3)
    all_keys = jax.random.split(key, REQS + 2)
    orders = jax.vmap(one_order)(all_keys[:REQS])
    group_count = MAXB // CAP
    common = jax.random.randint(all_keys[REQS], (), 0, N_REQ, dtype=jnp.int32)
    target = jax.random.randint(all_keys[REQS + 1], (REQS,), 0, group_count, dtype=jnp.int32)
    row_ids = jnp.arange(REQS, dtype=jnp.int32)
    where_common = jnp.argmax((orders == common).astype(jnp.int32), axis=1).astype(jnp.int32)
    moved = orders[row_ids, target]
    orders = orders.at[row_ids, where_common].set(moved)
    orders = orders.at[row_ids, target].set(common)
    orders = place_owner(orders, 0, N_REQ - 1, (target[0] + 1) % group_count, common)
    orders = place_owner(orders, 1, 0, (target[1] + 1) % group_count, common)
    slot_group = jnp.arange(MAXB, dtype=jnp.int32) // CAP
    return orders[:, slot_group]


def draw_block_index(key, part):
    key = jax.random.fold_in(key, 4)
    values = jax.random.randint(key, (REQS, MAXB), 0, NB_DEV, dtype=jnp.int32)
    return values.at[0, 0].set(NB_DEV - 1).at[0, 1].set(0)


def draw_prefix_blocks(key, part):
    key = jax.random.fold_in(key, 6)
    first_key, second_key = jax.random.split(key)
    lengths = jax.random.randint(first_key, (REQS,), 1, MAXB + 1, dtype=jnp.int32)
    longest = jax.random.randint(second_key, (), 0, REQS, dtype=jnp.int32)
    return lengths.at[longest].set(MAXB)


def draw_state_owner(key, part):
    key = jax.random.fold_in(key, 8)
    return jax.random.permutation(key, N_REQ).astype(jnp.int32)


def block_levels(rng, shape, pieces, smallest, largest):
    def one(dim, blocks):
        heights = jax.random.uniform(jax.random.fold_in(jax.random.fold_in(rng, 6), dim), (blocks,), jnp.float32, smallest / len(pieces), largest / len(pieces))
        return jnp.repeat(jnp.exp(heights), shape[dim] // blocks).reshape((-1,) + (1,) * (len(shape) - dim - 1))

    level = one(*pieces[0])
    for cut in pieces[1:]:
        level = level * one(*cut)
    return level


def noise(key, dims, spread, reach, shards=(), kind=jnp.bfloat16):
    level = block_levels(key, dims, shards, -0.22, 0.18) if shards else 1.0
    values = jax.random.normal(key, dims, jnp.float32) * spread * level
    return jnp.minimum(jnp.maximum(values, -reach), reach).astype(kind)


def setup_inputs(seed: int = 0, part: int = 0) -> dict:
    key_of = jax.random.split(jax.random.key(seed), 24)
    part_keys = jax.random.split(jax.random.fold_in(key_of[23], part), 24)
    queries = draw_queries(jax.random.fold_in(jax.random.fold_in(key_of[23], part), 71), part)
    kv_new = draw_kv_new(jax.random.fold_in(jax.random.fold_in(key_of[23], part), 71), part)
    kv_codes = noise(part_keys[2], (POOL, 2, KVH, BLK, HD), 1.0, 4.0, ((0, 4), (2, 4)))
    kv_scale = jnp.clip(jnp.exp(math.log(2.0) - 1.3862944 * jax.random.uniform(part_keys[3], (POOL, 2, KVH, BLK), jnp.float32) ** block_levels(part_keys[3], (POOL, 2, KVH, BLK), ((0, 4), (2, 4)), -0.2, 0.2)), 0.5, 2.0).astype(jnp.bfloat16)
    block_owner = draw_block_owner(jax.random.fold_in(jax.random.fold_in(key_of[23], part), 71), part)
    block_index = draw_block_index(jax.random.fold_in(jax.random.fold_in(key_of[23], part), 71), part)
    prefix_blocks = draw_prefix_blocks(jax.random.fold_in(jax.random.fold_in(key_of[23], part), 71), part)
    state_owner = draw_state_owner(jax.random.fold_in(jax.random.fold_in(key_of[23], part), 71), part)
    ssm_pool = noise(part_keys[8], (N_REQ, H, P_SIZE, N), N ** -0.5, 0.375, ((0, 4), (1, 4)), jnp.float32)
    conv_pool_x = noise(part_keys[9], (N_REQ, CONV_K - 1, H * P_SIZE), 1.0, 4.0, ((0, 4), (2, 4)))
    conv_pool_bc = noise(part_keys[10], (N_REQ, CONV_K - 1, 2, G * N), 1.0, 4.0, ((0, 4), (3, 4)))
    x_in = noise(part_keys[11], (REQS, L, H * P_SIZE), 1.0, 5.0, ((0, 4), (2, 4)))
    bc_in = noise(part_keys[12], (REQS, L, 2, G * N), 1.0, 5.0, ((0, 4), (3, 4)))
    z_in = noise(part_keys[13], (REQS, L, H * P_SIZE), 1.0, 5.0, ((0, 4), (2, 4)))
    dt_raw = noise(part_keys[14], (REQS, L, H), 1.0, 5.0, ((0, 4), (2, 4)), jnp.float32)
    dt_bias = jnp.clip(-4.0 + 2.0 * jax.random.uniform(key_of[15], (H,), jnp.float32) ** block_levels(key_of[15], (H,), ((0, 4),), -0.2, 0.2), -4.0, -2.0)
    ssm_rate = jnp.clip(jnp.exp(math.log(1.0) - 3.506558 * jax.random.uniform(key_of[16], (H,), jnp.float32) ** block_levels(key_of[16], (H,), ((0, 4),), -0.2, 0.2)), 0.03, 1.0)
    skip_gain = jnp.clip(0.5 + 1.0 * jax.random.uniform(key_of[17], (H,), jnp.float32) ** block_levels(key_of[17], (H,), ((0, 4),), -0.2, 0.2), 0.5, 1.5)
    conv_weight_x = noise(key_of[18], (CONV_K, H * P_SIZE), CONV_K ** -0.5, 3.0, ((1, 4),))
    conv_weight_bc = noise(key_of[19], (CONV_K, 2, G * N), CONV_K ** -0.5, 3.0, ((2, 4),))
    conv_bias_x = noise(key_of[20], (H * P_SIZE,), 0.5, 2.5, ((0, 4),))
    conv_bias_bc = noise(key_of[21], (2, G * N), 0.5, 2.5, ((1, 4),))
    norm_gain = jnp.clip(1.0 + 0.18 * jax.random.normal(key_of[22], (H * P_SIZE,), jnp.float32), 0.099609375, 1.8984375).astype(jnp.bfloat16)
    return {"queries": queries, "kv_new": kv_new, "kv_codes": kv_codes, "kv_scale": kv_scale, "block_owner": block_owner, "block_index": block_index, "prefix_blocks": prefix_blocks, "state_owner": state_owner, "ssm_pool": ssm_pool, "conv_pool_x": conv_pool_x, "conv_pool_bc": conv_pool_bc, "x_in": x_in, "bc_in": bc_in, "z_in": z_in, "dt_raw": dt_raw, "dt_bias": dt_bias, "ssm_rate": ssm_rate, "skip_gain": skip_gain, "conv_weight_x": conv_weight_x, "conv_weight_bc": conv_weight_bc, "conv_bias_x": conv_bias_x, "conv_bias_bc": conv_bias_bc, "norm_gain": norm_gain}


def hadamard_signs(order_len):
    index_row = jnp.arange(order_len, dtype=jnp.int32)
    common_bits = jnp.bitwise_and(index_row[:, None], index_row[None, :])
    parity = jnp.zeros((order_len, order_len), jnp.int32)
    for shift_by in range(max(order_len.bit_length() - 1, 0)):
        parity = parity + jnp.bitwise_and(jnp.right_shift(common_bits, shift_by), 1)
    return jnp.where(parity % 2 == 0, 1.0, -1.0).astype(jnp.bfloat16)

def dequantize(block_codes, scales, sign_table):
    row_width = block_codes.shape[-1]
    rotated = jnp.dot(block_codes.reshape(-1, row_width), sign_table, preferred_element_type=jnp.float32)
    rotated = rotated.reshape(block_codes.shape)
    return (rotated * scales.astype(jnp.float32)[..., None] * (1.0 / math.sqrt(row_width))).astype(jnp.bfloat16)

def causal_conv(history, incoming, weight, bias_row):
    joined = jnp.concatenate([history, incoming], axis=0).astype(jnp.float32)
    length = incoming.shape[0]
    summed = jnp.broadcast_to(bias_row.astype(jnp.float32), incoming.shape)
    for offset in range(weight.shape[0]):
        summed = summed + weight[offset].astype(jnp.float32) * joined[offset:offset + length]
    return jax.nn.silu(summed).astype(jnp.bfloat16)

def ssm_heads(conv_x, conv_bc, gate_rows, step_raw, dt_bias, ssm_rate, skip_gain, norm_gain, ssm_state):
    length, heads_here = step_raw.shape
    head_dim = ssm_state.shape[1]
    state_dim = ssm_state.shape[2]
    groups = conv_bc.shape[2] // state_dim
    per_group = heads_here // groups
    step_size = jax.nn.softplus(step_raw + dt_bias)
    cumulative = jnp.cumsum(-step_size * ssm_rate, axis=0)
    b_rows = conv_bc[:, 0].reshape(length, groups, state_dim).astype(jnp.float32)
    c_rows = conv_bc[:, 1].reshape(length, groups, state_dim).astype(jnp.float32)
    gram_rows = jnp.einsum('tgn,sgn->gts', c_rows, b_rows)
    by_head = cumulative.T
    log_decay = by_head[:, :, None] - by_head[:, None, :]
    position = jnp.arange(length)
    lower_mask = position[None, :] <= position[:, None]
    decay_mat = jnp.exp(jnp.where(lower_mask[None], log_decay, -jnp.inf))
    mix_rows = (gram_rows[:, None] * decay_mat.reshape(groups, per_group, length, length)).astype(jnp.bfloat16)
    mix_rows = lax.optimization_barrier(mix_rows).astype(jnp.float32)
    scaled_x = (conv_x.reshape(length, heads_here, head_dim).astype(jnp.float32) * step_size[:, :, None]).astype(jnp.bfloat16)
    scaled_x = lax.optimization_barrier(scaled_x).astype(jnp.float32)
    intra_term = jnp.einsum('gkts,sgkp->tgkp', mix_rows, scaled_x.reshape(length, groups, per_group, head_dim))
    carried = jnp.einsum('tgn,gkpn->tgkp', c_rows, ssm_state.reshape(groups, per_group, head_dim, state_dim), precision=lax.Precision.HIGHEST)
    carried = carried * jnp.exp(cumulative).reshape(length, groups, per_group)[..., None]
    x_heads = conv_x.reshape(length, groups, per_group, head_dim).astype(jnp.float32)
    y_heads = intra_term + carried + skip_gain.reshape(groups, per_group)[None, :, :, None] * x_heads
    gated = y_heads * jax.nn.silu(gate_rows.reshape(length, groups, per_group, head_dim).astype(jnp.float32))
    mean_square = lax.optimization_barrier(jnp.mean(gated * gated, axis=(2, 3), keepdims=True))
    normed = gated * lax.rsqrt(mean_square + 1e-05) * norm_gain.reshape(groups, per_group, head_dim).astype(jnp.float32)
    return normed.reshape(length, heads_here * head_dim).astype(jnp.bfloat16)

def attend(query_rows, new_rows, prefix, live_blocks):
    length, heads_all, head_width = query_rows.shape
    kv_heads = new_rows.shape[2]
    group_size = heads_all // kv_heads
    block_count = prefix.shape[0]
    score_scale = 1.0 / math.sqrt(head_width)
    grouped = query_rows.reshape(length, kv_heads, group_size, head_width).transpose(1, 0, 2, 3).astype(jnp.float32)
    key_pre = prefix[:, 0].transpose(1, 0, 2, 3).astype(jnp.float32)
    val_pre = prefix[:, 1].transpose(1, 0, 2, 3).astype(jnp.float32)
    key_new = new_rows[:, 0].transpose(1, 0, 2).astype(jnp.float32)
    val_new = new_rows[:, 1].transpose(1, 0, 2).astype(jnp.float32)
    position = jnp.arange(length)
    causal = position[None, :] <= position[:, None]
    live_mask = jnp.arange(block_count) < live_blocks

    def one_head(operands):
        head_q, head_kpre, head_vpre, head_knew, head_vnew = operands
        score_pre = jnp.einsum('tgd,jbd->gtjb', head_q, head_kpre) * score_scale
        score_new = jnp.einsum('tgd,sd->gts', head_q, head_knew) * score_scale
        score_pre = jnp.where(live_mask[None, None, :, None], score_pre, -jnp.inf)
        score_new = jnp.where(causal[None], score_new, -jnp.inf)
        row_max = jnp.maximum(lax.optimization_barrier(jnp.max(score_pre, axis=(2, 3))), lax.optimization_barrier(jnp.max(score_new, axis=2)))
        weight_pre = jnp.exp(score_pre - row_max[:, :, None, None])
        weight_new = jnp.exp(score_new - row_max[:, :, None])
        denominator = lax.optimization_barrier(jnp.sum(weight_pre, axis=(2, 3))) + lax.optimization_barrier(jnp.sum(weight_new, axis=2))
        rounded_pre = lax.optimization_barrier(weight_pre.astype(jnp.bfloat16)).astype(jnp.float32)
        rounded_new = lax.optimization_barrier(weight_new.astype(jnp.bfloat16)).astype(jnp.float32)
        numerator = jnp.einsum('gtjb,jbd->tgd', rounded_pre, head_vpre) + jnp.einsum('gts,sd->tgd', rounded_new, head_vnew)
        return (numerator / denominator.T[:, :, None]).astype(jnp.bfloat16)
    per_head = lax.map(one_head, (grouped, key_pre, val_pre, key_new, val_new))
    return per_head.transpose(1, 0, 2, 3).reshape(length, heads_all, head_width)

def reference(queries, kv_new, kv_codes, kv_scale, block_owner, block_index, prefix_blocks, state_owner, ssm_pool, conv_pool_x, conv_pool_bc, x_in, bc_in, z_in, dt_raw, dt_bias, ssm_rate, skip_gain, conv_weight_x, conv_weight_bc, conv_bias_x, conv_bias_bc, norm_gain):
    sign_table = hadamard_signs(HD)

    def one_request(request):
        cache_rows = (block_owner[request] * NB_DEV + block_index[request]).astype(jnp.int32)
        prefix = dequantize(kv_codes[cache_rows], kv_scale[cache_rows], sign_table)
        attended = attend(queries[request], kv_new[request], prefix, prefix_blocks[request])
        holder = state_owner[request]
        conv_x = causal_conv(conv_pool_x[holder], x_in[request], conv_weight_x, conv_bias_x)
        conv_bc = causal_conv(conv_pool_bc[holder], bc_in[request], conv_weight_bc, conv_bias_bc)
        ssm_rows = ssm_heads(conv_x, conv_bc, z_in[request], dt_raw[request], dt_bias, ssm_rate, skip_gain, norm_gain, ssm_pool[holder])
        return (ssm_rows, attended)
    ssm_out, attn_out = lax.map(one_request, jnp.arange(REQS, dtype=jnp.int32))
    return (ssm_out, attn_out)
```

```python
import functools
import math

import jax
import jax.numpy as jnp
from jax import lax
from jax.experimental import pallas as pl
from jax.experimental.pallas import tpu as pltpu
from jax.sharding import PartitionSpec as P

F32 = jnp.float32
BF16 = jnp.bfloat16
VMEM_LIMIT = 48 * 1024 * 1024


def hadamard_signs(order_len):
    index_row = jnp.arange(order_len, dtype=jnp.int32)
    common_bits = jnp.bitwise_and(index_row[:, None], index_row[None, :])
    parity = jnp.zeros((order_len, order_len), jnp.int32)
    for shift_by in range(max(order_len.bit_length() - 1, 0)):
        parity = parity + jnp.bitwise_and(jnp.right_shift(common_bits, shift_by), 1)
    return jnp.where(parity % 2 == 0, 1.0, -1.0).astype(BF16)


def dequantize(block_codes, scales, sign_table):
    row_width = block_codes.shape[-1]
    rotated = jnp.dot(
        block_codes.reshape(-1, row_width), sign_table, preferred_element_type=F32
    )
    rotated = rotated.reshape(block_codes.shape)
    return (rotated * scales.astype(F32)[..., None] * (1.0 / math.sqrt(row_width))).astype(BF16)


def causal_conv(history, incoming, weight, bias_row):
    joined = jnp.concatenate([history, incoming], axis=0).astype(F32)
    length = incoming.shape[0]
    summed = jnp.broadcast_to(bias_row.astype(F32), incoming.shape)
    for offset in range(weight.shape[0]):
        summed = summed + weight[offset].astype(F32) * joined[offset : offset + length]
    return jax.nn.silu(summed).astype(BF16)


def ssm_before_state(conv_x, conv_b, conv_c, step_raw, dt_bias, ssm_rate, skip_gain, state_dim):
    length, heads_here = step_raw.shape
    head_dim = conv_x.shape[1] // heads_here
    groups = conv_b.shape[1] // state_dim
    per_group = heads_here // groups
    step_size = jax.nn.softplus(step_raw + dt_bias)
    cumulative = jnp.cumsum(-step_size * ssm_rate, axis=0)
    b_rows = conv_b.reshape(length, groups, state_dim)
    c_rows = conv_c.reshape(length, groups, state_dim)
    gram_rows = jnp.einsum("tgn,sgn->gts", c_rows, b_rows, preferred_element_type=F32)
    by_head = cumulative.T
    log_decay = by_head[:, :, None] - by_head[:, None, :]
    position = jnp.arange(length)
    lower_mask = position[None, :] <= position[:, None]
    decay_mat = jnp.exp(jnp.where(lower_mask[None], log_decay, -jnp.inf))
    mix_rows = (gram_rows[:, None] * decay_mat.reshape(groups, per_group, length, length)).astype(
        BF16
    )
    x_heads = conv_x.reshape(length, heads_here, head_dim).astype(F32)
    scaled_x = (x_heads * step_size[:, :, None]).astype(BF16)
    intra_term = jnp.einsum(
        "gkts,sgkp->tgkp",
        mix_rows,
        scaled_x.reshape(length, groups, per_group, head_dim),
        preferred_element_type=F32,
    ).reshape(length, heads_here * head_dim)
    near = intra_term + jnp.repeat(skip_gain, head_dim)[None, :] * conv_x.astype(F32)
    decay = jnp.repeat(jnp.exp(cumulative), head_dim, axis=1)
    return near, decay


def tail_kernel(c_ref, state_ref, near_ref, decay_ref, z_ref, gain_ref, out_ref):
    carried = lax.dot_general(
        c_ref[...], state_ref[...], (((1,), (1,)), ((), ())), preferred_element_type=F32
    )
    y_heads = near_ref[...] + carried * decay_ref[...]
    gate = z_ref[...].astype(F32)
    gated = y_heads * (gate / (1.0 + jnp.exp(-gate)))
    mean_square = jnp.mean(gated * gated, axis=1, keepdims=True)
    out_ref[...] = (
        gated * lax.rsqrt(mean_square + 1e-05) * gain_ref[...].astype(F32)
    ).astype(BF16)


def ssm_tail(c_rows, state, near, decay, gate_rows, norm_gain):
    length, width = gate_rows.shape
    state_dim = state.shape[1]
    groups = c_rows.shape[1] // state_dim
    span = width // groups
    wide = pl.BlockSpec((length, span), lambda g: (0, g))
    return pl.pallas_call(
        tail_kernel,
        grid=(groups,),
        out_shape=jax.ShapeDtypeStruct((length, width), BF16),
        in_specs=[
            pl.BlockSpec((length, state_dim), lambda g: (0, g)),
            pl.BlockSpec((span, state_dim), lambda g: (g, 0)),
            wide,
            wide,
            wide,
            pl.BlockSpec((1, span), lambda g: (0, g)),
        ],
        out_specs=wide,
        compiler_params=pltpu.CompilerParams(vmem_limit_bytes=VMEM_LIMIT),
        cost_estimate=pl.CostEstimate(
            flops=2 * length * width * state_dim,
            bytes_accessed=length * width * 12 + width * state_dim * 2,
            transcendentals=length * width,
        ),
    )(c_rows, state, near, decay, gate_rows, norm_gain.reshape(1, -1))


def attend_kernel(rows_ref, live_ref, q_ref, new_ref, pool_ref, out_ref, key_buf, val_buf):
    kv_here = new_ref.shape[1]
    length = new_ref.shape[2]
    width = new_ref.shape[3]
    block_len = pool_ref.shape[3]
    table_len = rows_ref.shape[0]
    old_len = table_len * block_len
    tile, heads_here, _ = q_ref.shape
    share = heads_here // kv_here
    step = pl.program_id(0)

    @pl.when(step == 0)
    def _():
        def gather(entry, carry):
            row = rows_ref[entry]
            is_live = (entry < live_ref[0]).astype(F32)
            spot = pl.ds(pl.multiple_of(entry * block_len, block_len), block_len)
            for head in range(kv_here):
                key_buf[head, spot, :] = pool_ref[row, 0, head]
                values = pool_ref[row, 1, head].astype(F32) * is_live
                val_buf[head, spot, 0:width] = values.astype(BF16)
                val_buf[head, spot, width : 2 * width] = jnp.full(
                    (block_len, width), is_live, F32
                ).astype(BF16)
            return carry

        lax.fori_loop(0, table_len, gather, 0)
        for head in range(kv_here):
            key_buf[head, old_len : old_len + length, :] = new_ref[0, head]
            val_buf[head, old_len : old_len + length, 0:width] = new_ref[1, head]
            val_buf[head, old_len : old_len + length, width : 2 * width] = jnp.ones(
                (length, width), BF16
            )

    to_exp2 = math.log2(math.e) / math.sqrt(width)
    all_q = q_ref[...].astype(F32)
    count = tile * share
    row_id = lax.broadcasted_iota(jnp.int32, (count, length), 0)
    column = lax.broadcasted_iota(jnp.int32, (count, length), 1)
    causal = column * share <= row_id + step * count
    parts = []
    for head in range(kv_here):
        head_q = all_q[:, head * share : (head + 1) * share, :].reshape(count, width).astype(BF16)
        contract = (((1,), (1,)), ((), ()))
        score_old = lax.dot_general(
            head_q, key_buf[head, 0:old_len, :], contract, preferred_element_type=F32
        )
        score_new = lax.dot_general(
            head_q,
            key_buf[head, old_len : old_len + length, :],
            contract,
            preferred_element_type=F32,
        )
        score_new = jnp.where(causal, score_new, -jnp.inf)
        row_max = jnp.maximum(
            jnp.max(score_old, axis=1, keepdims=True), jnp.max(score_new, axis=1, keepdims=True)
        )
        weight_old = jnp.exp2((score_old - row_max) * to_exp2).astype(BF16)
        weight_new = jnp.exp2((score_new - row_max) * to_exp2).astype(BF16)
        total = jnp.dot(weight_old, val_buf[head, 0:old_len, :], preferred_element_type=F32)
        total = total + jnp.dot(
            weight_new,
            val_buf[head, old_len : old_len + length, :],
            preferred_element_type=F32,
        )
        parts.append((total[:, 0:width] / total[:, width : 2 * width]).reshape(tile, share, width))
    out_ref[...] = jnp.concatenate(parts, axis=1).astype(BF16)


def attend(query_rows, new_rows, pool, rows, live):
    length, heads_here, width = query_rows.shape
    kv_here = new_rows.shape[1]
    table_len = rows.shape[0]
    keys = table_len * pool.shape[3] + length
    tile = 32
    whole = lambda i, *_: (0, 0, 0, 0)
    return pl.pallas_call(
        attend_kernel,
        grid_spec=pltpu.PrefetchScalarGridSpec(
            num_scalar_prefetch=2,
            grid=(length // tile,),
            in_specs=[
                pl.BlockSpec((tile, heads_here, width), lambda i, *_: (i, 0, 0)),
                pl.BlockSpec(new_rows.shape, whole),
                pl.BlockSpec(memory_space=pltpu.VMEM),
            ],
            out_specs=pl.BlockSpec((tile, heads_here, width), lambda i, *_: (i, 0, 0)),
            scratch_shapes=[
                pltpu.VMEM((kv_here, keys, width), BF16),
                pltpu.VMEM((kv_here, keys, 2 * width), BF16),
            ],
        ),
        out_shape=jax.ShapeDtypeStruct(query_rows.shape, BF16),
        compiler_params=pltpu.CompilerParams(vmem_limit_bytes=VMEM_LIMIT),
        cost_estimate=pl.CostEstimate(
            flops=8 * length * heads_here * keys * width,
            bytes_accessed=pool.size * 2 + 4 * query_rows.size,
            transcendentals=length * heads_here * keys,
        ),
    )(rows, live, query_rows, new_rows, pool)


def body(
    queries,
    kv_new,
    kv_codes,
    kv_scale,
    block_owner,
    block_index,
    prefix_blocks,
    state_owner,
    ssm_pool,
    conv_pool_x,
    conv_pool_bc,
    x_in,
    bc_in,
    z_in,
    dt_raw,
    dt_bias,
    ssm_rate,
    skip_gain,
    conv_weight_x,
    conv_weight_bc,
    conv_bias_x,
    conv_bias_bc,
    norm_gain,
):
    owners = lax.axis_size("req")
    my_index = lax.axis_index("req")
    held = kv_codes.shape[0]
    state_dim = ssm_pool.shape[3]

    own_blocks = dequantize(kv_codes, kv_scale, hadamard_signs(kv_codes.shape[-1]))
    pool = lax.all_gather(own_blocks, "req", axis=0, tiled=True)

    taps = conv_pool_x.shape[1]
    rows_x = conv_pool_x.shape[2]
    rows_bc = conv_pool_bc.shape[3]
    history = jnp.concatenate(
        [conv_pool_x[0], conv_pool_bc[0, :, 0], conv_pool_bc[0, :, 1]], axis=1
    )
    all_history = lax.all_gather(history, "req", axis=0)
    my_source = lax.dynamic_index_in_dim(state_owner, my_index, 0, keepdims=False)
    my_history = lax.dynamic_index_in_dim(all_history, my_source, 0, keepdims=False)

    state_rows = ssm_pool[0].reshape(-1, state_dim).astype(BF16)
    spread = lax.all_to_all(state_rows, "req", split_axis=0, concat_axis=0, tiled=True)
    chosen = jnp.take(
        spread.reshape(owners, -1, state_dim), state_owner, axis=0, mode="clip"
    ).reshape(-1, state_dim)
    state = lax.all_to_all(chosen, "req", split_axis=0, concat_axis=0, tiled=True)

    conv_x = causal_conv(my_history[:, :rows_x], x_in[0], conv_weight_x, conv_bias_x)
    conv_b = causal_conv(
        my_history[:, rows_x : rows_x + rows_bc],
        bc_in[0, :, 0],
        conv_weight_bc[:, 0],
        conv_bias_bc[0],
    )
    conv_c = causal_conv(
        my_history[:, rows_x + rows_bc :], bc_in[0, :, 1], conv_weight_bc[:, 1], conv_bias_bc[1]
    )
    near, decay = ssm_before_state(
        conv_x, conv_b, conv_c, dt_raw[0], dt_bias, ssm_rate, skip_gain, state_dim
    )

    live = lax.dynamic_slice_in_dim(prefix_blocks, my_index, 1, 0)
    table = block_owner * held + block_index
    my_table = lax.dynamic_index_in_dim(table, my_index, 0, keepdims=False)
    rows = jnp.where(jnp.arange(my_table.shape[0]) < live, my_table, my_table[0])
    new_rows = kv_new[0].transpose(1, 2, 0, 3)
    attended = attend(queries[0], new_rows, pool, rows, live)

    ssm_rows = ssm_tail(conv_c, state, near, decay, z_in[0], norm_gain)
    return (ssm_rows[None], attended[None])


def solution(mesh):
    placed = (
        P(("grp", "req"), None, "tp", None),
        P(("grp", "req"), None, None, "tp", None),
        P(("grp", "req"), None, "tp", None, None),
        P(("grp", "req"), None, "tp", None),
        P("grp", None),
        P("grp", None),
        P("grp"),
        P("grp"),
        P(("grp", "req"), "tp", None, None),
        P(("grp", "req"), None, "tp"),
        P(("grp", "req"), None, None, "tp"),
        P(("grp", "req"), None, "tp"),
        P(("grp", "req"), None, None, "tp"),
        P(("grp", "req"), None, "tp"),
        P(("grp", "req"), None, "tp"),
        P("tp"),
        P("tp"),
        P("tp"),
        P(None, "tp"),
        P(None, None, "tp"),
        P("tp"),
        P(None, "tp"),
        P("tp"),
    )
    return jax.shard_map(
        body,
        mesh=mesh,
        in_specs=placed,
        out_specs=(P(("grp", "req"), None, "tp"), P(("grp", "req"), None, "tp", None)),
        check_vma=False,
    )
```

```python
import functools
import math

import jax
import jax.numpy as jnp
from jax import lax
from jax.experimental import pallas as pl
from jax.experimental.pallas import tpu as pltpu
from jax.sharding import PartitionSpec as P

F32 = jnp.float32
BF16 = jnp.bfloat16
VMEM_LIMIT = 48 * 1024 * 1024


def hadamard_signs(order_len):
    index_row = jnp.arange(order_len, dtype=jnp.int32)
    common_bits = jnp.bitwise_and(index_row[:, None], index_row[None, :])
    parity = jnp.zeros((order_len, order_len), jnp.int32)
    for shift_by in range(max(order_len.bit_length() - 1, 0)):
        parity = parity + jnp.bitwise_and(jnp.right_shift(common_bits, shift_by), 1)
    return jnp.where(parity % 2 == 0, 1.0, -1.0).astype(BF16)


def dequantize(block_codes, scales, sign_table):
    row_width = block_codes.shape[-1]
    rotated = jnp.dot(
        block_codes.reshape(-1, row_width), sign_table, preferred_element_type=F32
    )
    rotated = rotated.reshape(block_codes.shape)
    return (rotated * scales.astype(F32)[..., None] * (1.0 / math.sqrt(row_width))).astype(BF16)


def causal_conv(history, incoming, weight, bias_row):
    joined = jnp.concatenate([history, incoming], axis=0).astype(F32)
    length = incoming.shape[0]
    summed = jnp.broadcast_to(bias_row.astype(F32), incoming.shape)
    for offset in range(weight.shape[0]):
        summed = summed + weight[offset].astype(F32) * joined[offset : offset + length]
    return jax.nn.silu(summed).astype(BF16)


def ssm_before_state(conv_x, conv_b, conv_c, step_raw, dt_bias, ssm_rate, skip_gain, state_dim):
    length, heads_here = step_raw.shape
    head_dim = conv_x.shape[1] // heads_here
    groups = conv_b.shape[1] // state_dim
    per_group = heads_here // groups
    step_size = jax.nn.softplus(step_raw + dt_bias)
    cumulative = jnp.cumsum(-step_size * ssm_rate, axis=0)
    b_rows = conv_b.reshape(length, groups, state_dim)
    c_rows = conv_c.reshape(length, groups, state_dim)
    gram_rows = jnp.einsum("tgn,sgn->gts", c_rows, b_rows, preferred_element_type=F32)
    by_head = cumulative.T
    log_decay = by_head[:, :, None] - by_head[:, None, :]
    position = jnp.arange(length)
    lower_mask = position[None, :] <= position[:, None]
    decay_mat = jnp.exp(jnp.where(lower_mask[None], log_decay, -jnp.inf))
    mix_rows = (gram_rows[:, None] * decay_mat.reshape(groups, per_group, length, length)).astype(
        BF16
    )
    x_heads = conv_x.reshape(length, heads_here, head_dim).astype(F32)
    scaled_x = (x_heads * step_size[:, :, None]).astype(BF16)
    intra_term = jnp.einsum(
        "gkts,sgkp->tgkp",
        mix_rows,
        scaled_x.reshape(length, groups, per_group, head_dim),
        preferred_element_type=F32,
    ).reshape(length, heads_here * head_dim)
    near = intra_term + jnp.repeat(skip_gain, head_dim)[None, :] * conv_x.astype(F32)
    decay = jnp.repeat(jnp.exp(cumulative), head_dim, axis=1)
    return near, decay


def tail_kernel(c_ref, state_ref, near_ref, decay_ref, z_ref, gain_ref, after_ref, out_ref):
    carried = lax.dot_general(
        c_ref[...], state_ref[...], (((1,), (1,)), ((), ())), preferred_element_type=F32
    )
    y_heads = near_ref[...] + carried * decay_ref[...]
    gate = z_ref[...].astype(F32)
    gated = y_heads * (gate / (1.0 + jnp.exp(-gate)))
    mean_square = jnp.mean(gated * gated, axis=1, keepdims=True)
    out_ref[...] = (
        gated * lax.rsqrt(mean_square + 1e-05) * gain_ref[...].astype(F32)
    ).astype(BF16)


def ssm_tail(c_rows, state, near, decay, gate_rows, norm_gain, after):
    length, width = gate_rows.shape
    state_dim = state.shape[1]
    groups = c_rows.shape[1] // state_dim
    span = width // groups
    wide = pl.BlockSpec((length, span), lambda g: (0, g))
    return pl.pallas_call(
        tail_kernel,
        grid=(groups,),
        out_shape=jax.ShapeDtypeStruct((length, width), BF16),
        in_specs=[
            pl.BlockSpec((length, state_dim), lambda g: (0, g)),
            pl.BlockSpec((span, state_dim), lambda g: (g, 0)),
            wide,
            wide,
            wide,
            pl.BlockSpec((1, span), lambda g: (0, g)),
            pl.BlockSpec(memory_space=pl.ANY),
        ],
        out_specs=wide,
        compiler_params=pltpu.CompilerParams(vmem_limit_bytes=VMEM_LIMIT),
        cost_estimate=pl.CostEstimate(
            flops=2 * length * width * state_dim,
            bytes_accessed=length * width * 12 + width * state_dim * 2,
            transcendentals=length * width,
        ),
    )(c_rows, state, near, decay, gate_rows, norm_gain.reshape(1, -1), after)


def choose_kernel(owner_ref, piece_ref, pool_ref, near_ref, out_ref):
    out_ref[...] = piece_ref[...]


def choose_pieces(state_owner, spread, piece_rows, pool, near):
    owners, _, state_dim = spread.shape
    block = (1, piece_rows, state_dim)
    return pl.pallas_call(
        choose_kernel,
        grid_spec=pltpu.PrefetchScalarGridSpec(
            num_scalar_prefetch=1,
            grid=(owners,),
            in_specs=[
                pl.BlockSpec(block, lambda i, owner: (owner[i], 0, 0)),
                pl.BlockSpec(memory_space=pl.ANY),
                pl.BlockSpec(memory_space=pl.ANY),
            ],
            out_specs=pl.BlockSpec(block, lambda i, owner: (i, 0, 0)),
        ),
        out_shape=jax.ShapeDtypeStruct((owners, piece_rows, state_dim), BF16),
        compiler_params=pltpu.CompilerParams(vmem_limit_bytes=VMEM_LIMIT),
    )(state_owner, spread, pool, near)


def attend_kernel(
    rows_ref, live_ref, q_ref, new_ref, pool_ref, after_ref, out_ref, key_buf, val_buf
):
    kv_here = new_ref.shape[1]
    length = new_ref.shape[2]
    width = new_ref.shape[3]
    block_len = pool_ref.shape[3]
    table_len = rows_ref.shape[0]
    old_len = table_len * block_len
    tile, heads_here, _ = q_ref.shape
    share = heads_here // kv_here
    step = pl.program_id(0)

    @pl.when(step == 0)
    def _():
        def gather(entry, carry):
            row = rows_ref[entry]
            is_live = (entry < live_ref[0]).astype(F32)
            spot = pl.ds(pl.multiple_of(entry * block_len, block_len), block_len)
            for head in range(kv_here):
                key_buf[head, spot, :] = pool_ref[row, 0, head]
                values = pool_ref[row, 1, head].astype(F32) * is_live
                val_buf[head, spot, 0:width] = values.astype(BF16)
                val_buf[head, spot, width : 2 * width] = jnp.full(
                    (block_len, width), is_live, F32
                ).astype(BF16)
            return carry

        lax.fori_loop(0, table_len, gather, 0)
        for head in range(kv_here):
            key_buf[head, old_len : old_len + length, :] = new_ref[0, head]
            val_buf[head, old_len : old_len + length, 0:width] = new_ref[1, head]
            val_buf[head, old_len : old_len + length, width : 2 * width] = jnp.ones(
                (length, width), BF16
            )

    to_exp2 = math.log2(math.e) / math.sqrt(width)
    all_q = q_ref[...].astype(F32)
    count = tile * share
    row_id = lax.broadcasted_iota(jnp.int32, (count, length), 0)
    column = lax.broadcasted_iota(jnp.int32, (count, length), 1)
    causal = column * share <= row_id + step * count
    parts = []
    for head in range(kv_here):
        head_q = all_q[:, head * share : (head + 1) * share, :].reshape(count, width).astype(BF16)
        contract = (((1,), (1,)), ((), ()))
        score_old = lax.dot_general(
            head_q, key_buf[head, 0:old_len, :], contract, preferred_element_type=F32
        )
        score_new = lax.dot_general(
            head_q,
            key_buf[head, old_len : old_len + length, :],
            contract,
            preferred_element_type=F32,
        )
        score_new = jnp.where(causal, score_new, -jnp.inf)
        row_max = jnp.maximum(
            jnp.max(score_old, axis=1, keepdims=True), jnp.max(score_new, axis=1, keepdims=True)
        )
        weight_old = jnp.exp2((score_old - row_max) * to_exp2).astype(BF16)
        weight_new = jnp.exp2((score_new - row_max) * to_exp2).astype(BF16)
        total = jnp.dot(weight_old, val_buf[head, 0:old_len, :], preferred_element_type=F32)
        total = total + jnp.dot(
            weight_new,
            val_buf[head, old_len : old_len + length, :],
            preferred_element_type=F32,
        )
        parts.append((total[:, 0:width] / total[:, width : 2 * width]).reshape(tile, share, width))
    out_ref[...] = jnp.concatenate(parts, axis=1).astype(BF16)


def attend(query_rows, new_rows, pool, rows, live, after):
    length, heads_here, width = query_rows.shape
    kv_here = new_rows.shape[1]
    table_len = rows.shape[0]
    keys = table_len * pool.shape[3] + length
    tile = 32
    whole = lambda i, *_: (0, 0, 0, 0)
    return pl.pallas_call(
        attend_kernel,
        grid_spec=pltpu.PrefetchScalarGridSpec(
            num_scalar_prefetch=2,
            grid=(length // tile,),
            in_specs=[
                pl.BlockSpec((tile, heads_here, width), lambda i, *_: (i, 0, 0)),
                pl.BlockSpec(new_rows.shape, whole),
                pl.BlockSpec(memory_space=pltpu.VMEM),
                pl.BlockSpec(memory_space=pl.ANY),
            ],
            out_specs=pl.BlockSpec((tile, heads_here, width), lambda i, *_: (i, 0, 0)),
            scratch_shapes=[
                pltpu.VMEM((kv_here, keys, width), BF16),
                pltpu.VMEM((kv_here, keys, 2 * width), BF16),
            ],
        ),
        out_shape=jax.ShapeDtypeStruct(query_rows.shape, BF16),
        compiler_params=pltpu.CompilerParams(vmem_limit_bytes=VMEM_LIMIT),
        cost_estimate=pl.CostEstimate(
            flops=8 * length * heads_here * keys * width,
            bytes_accessed=pool.size * 2 + 4 * query_rows.size,
            transcendentals=length * heads_here * keys,
        ),
    )(rows, live, query_rows, new_rows, pool, after)


def body(
    queries,
    kv_new,
    kv_codes,
    kv_scale,
    block_owner,
    block_index,
    prefix_blocks,
    state_owner,
    ssm_pool,
    conv_pool_x,
    conv_pool_bc,
    x_in,
    bc_in,
    z_in,
    dt_raw,
    dt_bias,
    ssm_rate,
    skip_gain,
    conv_weight_x,
    conv_weight_bc,
    conv_bias_x,
    conv_bias_bc,
    norm_gain,
):
    owners = lax.axis_size("req")
    my_index = lax.axis_index("req")
    held = kv_codes.shape[0]
    state_dim = ssm_pool.shape[3]

    own_blocks = dequantize(kv_codes, kv_scale, hadamard_signs(kv_codes.shape[-1]))
    pool = lax.all_gather(own_blocks, "req", axis=0, tiled=True)

    taps = conv_pool_x.shape[1]
    rows_x = conv_pool_x.shape[2]
    rows_bc = conv_pool_bc.shape[3]
    history = jnp.concatenate(
        [conv_pool_x[0], conv_pool_bc[0, :, 0], conv_pool_bc[0, :, 1]], axis=1
    )
    flat_rows = -(-history.size // state_dim)
    pad_rows = -(-flat_rows // 16) * 16
    flat_history = jnp.pad(history.reshape(-1), (0, pad_rows * state_dim - history.size))
    state_pieces = ssm_pool[0].astype(BF16).reshape(owners, -1, state_dim)
    piece_rows = state_pieces.shape[1]
    outgoing = jnp.concatenate(
        [
            state_pieces,
            jnp.broadcast_to(
                flat_history.reshape(1, pad_rows, state_dim), (owners, pad_rows, state_dim)
            ),
        ],
        axis=1,
    )
    spread = lax.all_to_all(outgoing, "req", split_axis=0, concat_axis=0, tiled=True)
    my_source = lax.dynamic_index_in_dim(state_owner, my_index, 0, keepdims=False)
    my_history = lax.dynamic_slice(
        spread, (my_source, piece_rows, 0), (1, pad_rows, state_dim)
    ).reshape(-1)[: history.size].reshape(history.shape)

    conv_x = causal_conv(my_history[:, :rows_x], x_in[0], conv_weight_x, conv_bias_x)
    conv_b = causal_conv(
        my_history[:, rows_x : rows_x + rows_bc],
        bc_in[0, :, 0],
        conv_weight_bc[:, 0],
        conv_bias_bc[0],
    )
    conv_c = causal_conv(
        my_history[:, rows_x + rows_bc :], bc_in[0, :, 1], conv_weight_bc[:, 1], conv_bias_bc[1]
    )
    near, decay = ssm_before_state(
        conv_x, conv_b, conv_c, dt_raw[0], dt_bias, ssm_rate, skip_gain, state_dim
    )

    chosen = choose_pieces(state_owner, spread, piece_rows, pool, near)
    state = lax.all_to_all(chosen, "req", split_axis=0, concat_axis=0, tiled=True)
    state = state.reshape(-1, state_dim)

    live = lax.dynamic_slice_in_dim(prefix_blocks, my_index, 1, 0)
    table = block_owner * held + block_index
    my_table = lax.dynamic_index_in_dim(table, my_index, 0, keepdims=False)
    rows = jnp.where(jnp.arange(my_table.shape[0]) < live, my_table, my_table[0])
    new_rows = kv_new[0].transpose(1, 2, 0, 3)
    attended = attend(queries[0], new_rows, pool, rows, live, chosen)

    ssm_rows = ssm_tail(conv_c, state, near, decay, z_in[0], norm_gain, attended)
    return (ssm_rows[None], attended[None])


def solution(mesh):
    placed = (
        P(("grp", "req"), None, "tp", None),
        P(("grp", "req"), None, None, "tp", None),
        P(("grp", "req"), None, "tp", None, None),
        P(("grp", "req"), None, "tp", None),
        P("grp", None),
        P("grp", None),
        P("grp"),
        P("grp"),
        P(("grp", "req"), "tp", None, None),
        P(("grp", "req"), None, "tp"),
        P(("grp", "req"), None, None, "tp"),
        P(("grp", "req"), None, "tp"),
        P(("grp", "req"), None, None, "tp"),
        P(("grp", "req"), None, "tp"),
        P(("grp", "req"), None, "tp"),
        P("tp"),
        P("tp"),
        P("tp"),
        P(None, "tp"),
        P(None, None, "tp"),
        P("tp"),
        P(None, "tp"),
        P("tp"),
    )
    return jax.shard_map(
        body,
        mesh=mesh,
        in_specs=placed,
        out_specs=(P(("grp", "req"), None, "tp"), P(("grp", "req"), None, "tp", None)),
        check_vma=False,
    )
```

```python
import functools
import math

import jax
import jax.numpy as jnp
from jax import lax
from jax.experimental import pallas as pl
from jax.experimental.pallas import tpu as pltpu
from jax.sharding import PartitionSpec as P

F32 = jnp.float32
BF16 = jnp.bfloat16
VMEM_LIMIT = 48 * 1024 * 1024


def hadamard_signs(order_len):
    index_row = jnp.arange(order_len, dtype=jnp.int32)
    common_bits = jnp.bitwise_and(index_row[:, None], index_row[None, :])
    parity = jnp.zeros((order_len, order_len), jnp.int32)
    for shift_by in range(max(order_len.bit_length() - 1, 0)):
        parity = parity + jnp.bitwise_and(jnp.right_shift(common_bits, shift_by), 1)
    return jnp.where(parity % 2 == 0, 1.0, -1.0).astype(BF16)


def dequantize(block_codes, scales, sign_table):
    row_width = block_codes.shape[-1]
    rotated = jnp.dot(
        block_codes.reshape(-1, row_width), sign_table, preferred_element_type=F32
    )
    rotated = rotated.reshape(block_codes.shape)
    return (rotated * scales.astype(F32)[..., None] * (1.0 / math.sqrt(row_width))).astype(BF16)


def causal_conv(history, incoming, weight, bias_row):
    joined = jnp.concatenate([history, incoming], axis=0).astype(F32)
    length = incoming.shape[0]
    summed = jnp.broadcast_to(bias_row.astype(F32), incoming.shape)
    for offset in range(weight.shape[0]):
        summed = summed + weight[offset].astype(F32) * joined[offset : offset + length]
    return jax.nn.silu(summed).astype(BF16)


def ssm_before_state(conv_x, conv_b, conv_c, step_raw, dt_bias, ssm_rate, skip_gain, state_dim):
    length, heads_here = step_raw.shape
    head_dim = conv_x.shape[1] // heads_here
    groups = conv_b.shape[1] // state_dim
    per_group = heads_here // groups
    step_size = jax.nn.softplus(step_raw + dt_bias)
    cumulative = jnp.cumsum(-step_size * ssm_rate, axis=0)
    b_rows = conv_b.reshape(length, groups, state_dim)
    c_rows = conv_c.reshape(length, groups, state_dim)
    gram_rows = jnp.einsum("tgn,sgn->gts", c_rows, b_rows, preferred_element_type=F32)
    by_head = cumulative.T
    log_decay = by_head[:, :, None] - by_head[:, None, :]
    position = jnp.arange(length)
    lower_mask = position[None, :] <= position[:, None]
    decay_mat = jnp.exp(jnp.where(lower_mask[None], log_decay, -jnp.inf))
    mix_rows = (gram_rows[:, None] * decay_mat.reshape(groups, per_group, length, length)).astype(
        BF16
    )
    x_heads = conv_x.reshape(length, heads_here, head_dim).astype(F32)
    scaled_x = (x_heads * step_size[:, :, None]).astype(BF16)
    intra_term = jnp.einsum(
        "gkts,sgkp->tgkp",
        mix_rows,
        scaled_x.reshape(length, groups, per_group, head_dim),
        preferred_element_type=F32,
    ).reshape(length, heads_here * head_dim)
    near = intra_term + jnp.repeat(skip_gain, head_dim)[None, :] * conv_x.astype(F32)
    decay = jnp.repeat(jnp.exp(cumulative), head_dim, axis=1)
    return near, decay


def tail_kernel(c_ref, state_ref, near_ref, decay_ref, z_ref, gain_ref, after_ref, out_ref):
    carried = lax.dot_general(
        c_ref[...], state_ref[...], (((1,), (1,)), ((), ())), preferred_element_type=F32
    )
    y_heads = near_ref[...] + carried * decay_ref[...]
    gate = z_ref[...].astype(F32)
    gated = y_heads * (gate / (1.0 + jnp.exp(-gate)))
    mean_square = jnp.mean(gated * gated, axis=1, keepdims=True)
    out_ref[...] = (
        gated * lax.rsqrt(mean_square + 1e-05) * gain_ref[...].astype(F32)
    ).astype(BF16)


def ssm_tail(c_rows, state, near, decay, gate_rows, norm_gain, after):
    length, width = gate_rows.shape
    state_dim = state.shape[1]
    groups = c_rows.shape[1] // state_dim
    span = width // groups
    wide = pl.BlockSpec((length, span), lambda g: (0, g))
    return pl.pallas_call(
        tail_kernel,
        grid=(groups,),
        out_shape=jax.ShapeDtypeStruct((length, width), BF16),
        in_specs=[
            pl.BlockSpec((length, state_dim), lambda g: (0, g)),
            pl.BlockSpec((span, state_dim), lambda g: (g, 0)),
            wide,
            wide,
            wide,
            pl.BlockSpec((1, span), lambda g: (0, g)),
            pl.BlockSpec(memory_space=pl.ANY),
        ],
        out_specs=wide,
        compiler_params=pltpu.CompilerParams(vmem_limit_bytes=VMEM_LIMIT),
        cost_estimate=pl.CostEstimate(
            flops=2 * length * width * state_dim,
            bytes_accessed=length * width * 12 + width * state_dim * 2,
            transcendentals=length * width,
        ),
    )(c_rows, state, near, decay, gate_rows, norm_gain.reshape(1, -1), after)


def choose_kernel(owner_ref, piece_ref, *refs):
    out_ref = refs[-1]
    out_ref[...] = piece_ref[...]


def choose_pieces(state_owner, spread, piece_rows, *before):
    owners, _, state_dim = spread.shape
    block = (1, piece_rows, state_dim)
    return pl.pallas_call(
        choose_kernel,
        grid_spec=pltpu.PrefetchScalarGridSpec(
            num_scalar_prefetch=1,
            grid=(owners,),
            in_specs=[
                pl.BlockSpec(block, lambda i, owner: (owner[i], 0, 0)),
            ]
            + [pl.BlockSpec(memory_space=pl.ANY)] * len(before),
            out_specs=pl.BlockSpec(block, lambda i, owner: (i, 0, 0)),
        ),
        out_shape=jax.ShapeDtypeStruct((owners, piece_rows, state_dim), BF16),
        compiler_params=pltpu.CompilerParams(vmem_limit_bytes=VMEM_LIMIT),
    )(state_owner, spread, *before)


def attend_kernel(
    rows_ref, live_ref, q_ref, new_ref, pool_ref, after_ref, out_ref, key_buf, val_buf
):
    kv_here = new_ref.shape[1]
    length = new_ref.shape[2]
    width = new_ref.shape[3]
    block_len = pool_ref.shape[3]
    table_len = rows_ref.shape[0]
    old_len = table_len * block_len
    tile, heads_here, _ = q_ref.shape
    share = heads_here // kv_here
    step = pl.program_id(0)

    @pl.when(step == 0)
    def _():
        def gather(entry, carry):
            row = rows_ref[entry]
            is_live = (entry < live_ref[0]).astype(F32)
            spot = pl.ds(pl.multiple_of(entry * block_len, block_len), block_len)
            for head in range(kv_here):
                key_buf[head, spot, :] = pool_ref[row, 0, head]
                values = pool_ref[row, 1, head].astype(F32) * is_live
                val_buf[head, spot, 0:width] = values.astype(BF16)
                val_buf[head, spot, width : 2 * width] = jnp.full(
                    (block_len, width), is_live, F32
                ).astype(BF16)
            return carry

        lax.fori_loop(0, table_len, gather, 0)
        for head in range(kv_here):
            key_buf[head, old_len : old_len + length, :] = new_ref[0, head]
            val_buf[head, old_len : old_len + length, 0:width] = new_ref[1, head]
            val_buf[head, old_len : old_len + length, width : 2 * width] = jnp.ones(
                (length, width), BF16
            )

    to_exp2 = math.log2(math.e) / math.sqrt(width)
    all_q = q_ref[...].astype(F32)
    count = tile * share
    row_id = lax.broadcasted_iota(jnp.int32, (count, length), 0)
    column = lax.broadcasted_iota(jnp.int32, (count, length), 1)
    causal = column * share <= row_id + step * count
    parts = []
    for head in range(kv_here):
        head_q = all_q[:, head * share : (head + 1) * share, :].reshape(count, width).astype(BF16)
        contract = (((1,), (1,)), ((), ()))
        score_old = lax.dot_general(
            head_q, key_buf[head, 0:old_len, :], contract, preferred_element_type=F32
        )
        score_new = lax.dot_general(
            head_q,
            key_buf[head, old_len : old_len + length, :],
            contract,
            preferred_element_type=F32,
        )
        score_new = jnp.where(causal, score_new, -jnp.inf)
        row_max = jnp.maximum(
            jnp.max(score_old, axis=1, keepdims=True), jnp.max(score_new, axis=1, keepdims=True)
        )
        weight_old = jnp.exp2((score_old - row_max) * to_exp2).astype(BF16)
        weight_new = jnp.exp2((score_new - row_max) * to_exp2).astype(BF16)
        total = jnp.dot(weight_old, val_buf[head, 0:old_len, :], preferred_element_type=F32)
        total = total + jnp.dot(
            weight_new,
            val_buf[head, old_len : old_len + length, :],
            preferred_element_type=F32,
        )
        parts.append((total[:, 0:width] / total[:, width : 2 * width]).reshape(tile, share, width))
    out_ref[...] = jnp.concatenate(parts, axis=1).astype(BF16)


def attend(query_rows, new_rows, pool, rows, live, after):
    length, heads_here, width = query_rows.shape
    kv_here = new_rows.shape[1]
    table_len = rows.shape[0]
    keys = table_len * pool.shape[3] + length
    tile = 32
    whole = lambda i, *_: (0, 0, 0, 0)
    return pl.pallas_call(
        attend_kernel,
        grid_spec=pltpu.PrefetchScalarGridSpec(
            num_scalar_prefetch=2,
            grid=(length // tile,),
            in_specs=[
                pl.BlockSpec((tile, heads_here, width), lambda i, *_: (i, 0, 0)),
                pl.BlockSpec(new_rows.shape, whole),
                pl.BlockSpec(memory_space=pltpu.VMEM),
                pl.BlockSpec(memory_space=pl.ANY),
            ],
            out_specs=pl.BlockSpec((tile, heads_here, width), lambda i, *_: (i, 0, 0)),
            scratch_shapes=[
                pltpu.VMEM((kv_here, keys, width), BF16),
                pltpu.VMEM((kv_here, keys, 2 * width), BF16),
            ],
        ),
        out_shape=jax.ShapeDtypeStruct(query_rows.shape, BF16),
        compiler_params=pltpu.CompilerParams(vmem_limit_bytes=VMEM_LIMIT),
        cost_estimate=pl.CostEstimate(
            flops=8 * length * heads_here * keys * width,
            bytes_accessed=pool.size * 2 + 4 * query_rows.size,
            transcendentals=length * heads_here * keys,
        ),
    )(rows, live, query_rows, new_rows, pool, after)


def body(
    queries,
    kv_new,
    kv_codes,
    kv_scale,
    block_owner,
    block_index,
    prefix_blocks,
    state_owner,
    ssm_pool,
    conv_pool_x,
    conv_pool_bc,
    x_in,
    bc_in,
    z_in,
    dt_raw,
    dt_bias,
    ssm_rate,
    skip_gain,
    conv_weight_x,
    conv_weight_bc,
    conv_bias_x,
    conv_bias_bc,
    norm_gain,
):
    owners = lax.axis_size("req")
    my_index = lax.axis_index("req")
    held = kv_codes.shape[0]
    state_dim = ssm_pool.shape[3]

    own_blocks = dequantize(kv_codes, kv_scale, hadamard_signs(kv_codes.shape[-1]))
    pool = lax.all_gather(own_blocks, "req", axis=0, tiled=True)

    taps = conv_pool_x.shape[1]
    rows_x = conv_pool_x.shape[2]
    rows_bc = conv_pool_bc.shape[3]
    history = jnp.concatenate(
        [conv_pool_x[0], conv_pool_bc[0, :, 0], conv_pool_bc[0, :, 1]], axis=1
    )
    flat_rows = -(-history.size // state_dim)
    pad_rows = -(-flat_rows // 16) * 16
    flat_history = jnp.pad(history.reshape(-1), (0, pad_rows * state_dim - history.size))
    state_pieces = ssm_pool[0].astype(BF16).reshape(owners, -1, state_dim)
    piece_rows = state_pieces.shape[1]
    outgoing = jnp.concatenate(
        [
            state_pieces,
            jnp.broadcast_to(
                flat_history.reshape(1, pad_rows, state_dim), (owners, pad_rows, state_dim)
            ),
        ],
        axis=1,
    )
    spread = lax.all_to_all(outgoing, "req", split_axis=0, concat_axis=0, tiled=True)
    my_source = lax.dynamic_index_in_dim(state_owner, my_index, 0, keepdims=False)
    my_history = lax.dynamic_slice(
        spread, (my_source, piece_rows, 0), (1, pad_rows, state_dim)
    ).reshape(-1)[: history.size].reshape(history.shape)

    conv_x = causal_conv(my_history[:, :rows_x], x_in[0], conv_weight_x, conv_bias_x)
    conv_b = causal_conv(
        my_history[:, rows_x : rows_x + rows_bc],
        bc_in[0, :, 0],
        conv_weight_bc[:, 0],
        conv_bias_bc[0],
    )
    conv_c = causal_conv(
        my_history[:, rows_x + rows_bc :], bc_in[0, :, 1], conv_weight_bc[:, 1], conv_bias_bc[1]
    )
    near, decay = ssm_before_state(
        conv_x, conv_b, conv_c, dt_raw[0], dt_bias, ssm_rate, skip_gain, state_dim
    )

    live = lax.dynamic_slice_in_dim(prefix_blocks, my_index, 1, 0)
    table = block_owner * held + block_index
    my_table = lax.dynamic_index_in_dim(table, my_index, 0, keepdims=False)
    rows = jnp.where(jnp.arange(my_table.shape[0]) < live, my_table, my_table[0])
    new_rows = kv_new[0].transpose(1, 2, 0, 3)
    chosen = choose_pieces(state_owner, spread, piece_rows, pool, near, decay, new_rows, rows)
    state = lax.all_to_all(chosen, "req", split_axis=0, concat_axis=0, tiled=True)
    state = state.reshape(-1, state_dim)
    attended = attend(queries[0], new_rows, pool, rows, live, chosen)

    ssm_rows = ssm_tail(conv_c, state, near, decay, z_in[0], norm_gain, attended)
    return (ssm_rows[None], attended[None])


def solution(mesh):
    placed = (
        P(("grp", "req"), None, "tp", None),
        P(("grp", "req"), None, None, "tp", None),
        P(("grp", "req"), None, "tp", None, None),
        P(("grp", "req"), None, "tp", None),
        P("grp", None),
        P("grp", None),
        P("grp"),
        P("grp"),
        P(("grp", "req"), "tp", None, None),
        P(("grp", "req"), None, "tp"),
        P(("grp", "req"), None, None, "tp"),
        P(("grp", "req"), None, "tp"),
        P(("grp", "req"), None, None, "tp"),
        P(("grp", "req"), None, "tp"),
        P(("grp", "req"), None, "tp"),
        P("tp"),
        P("tp"),
        P("tp"),
        P(None, "tp"),
        P(None, None, "tp"),
        P("tp"),
        P(None, "tp"),
        P("tp"),
    )
    return jax.shard_map(
        body,
        mesh=mesh,
        in_specs=placed,
        out_specs=(P(("grp", "req"), None, "tp"), P(("grp", "req"), None, "tp", None)),
        check_vma=False,
    )
```
